32 devices in a mesh: groups: 2 (over y), gallery: 4 (over z), query: 4 (over x, core).
Axes of the slice: x: 2, y: 2, z: 4, core: 2. Of those that a mesh axis runs over, the one named last changes fastest.
Arguments:
- gallery: bfloat16 [2048, 2048], P(('groups', 'gallery'), 'query'), parts along dimension 0
- neighbour: int32 [2048, 10], P(('groups', 'gallery')), parts along dimension 0, may hold values from 0 to 319, as said below
- weights: int32 [2048, 10], P(('groups', 'gallery')), parts along dimension 0, may hold values from 1 to 4
- send_rows: int32 [8, 64], P(('groups', 'gallery')), parts along dimension 0, may hold values from 0 to 255, as said below
- queries: bfloat16 [1024, 2048], P('gallery', 'query'), may hold values from -6 to 6
Outputs:
- refined: bfloat16 [2048, 2048], P(('groups', 'gallery'), 'query'), parts along dimension 0
- scores: bfloat16 [2048, 1024], P(('groups', 'gallery'), 'query'), parts along dimension 0
The draws below stay inside these ranges and needn't reach their ends.
There are 2 independent parts, one for each index of `groups`. The reference program is written for one: setup_inputs(seed, part) draws one part's arguments, and reference() takes and returns one part's arrays. A program takes and returns all parts, laid end to end along the dimension named above; an argument that names none is the same for every part. Nothing has to cross between parts.
Inputs may be any that keep to these rules, and one draw needn't show every extreme that they name: `neighbour`: A value below 256 names a row of the row's own shard. A value v of 256 or more names position (v - 256) % 16 of the list that shard (v - 256) // 16 sends to the row's shard, never the shard's own list. `send_rows`: row s, positions d * 16 to d * 16 + 15: rows of shard s, numbered within the shard, listed for shard d, all different.
All inputs are finite; a program needn't handle non-finite values.
Results may differ from the reference program's by a relative error of at most 0.0049.
Values may be sent and summed in bfloat16 or wider, within the bound.
No kernel may reach another device: no remote copies, remote signals or barrier semaphores. Data moves between devices by JAX's collectives and lax.ppermute only.
A program may use at most 64 MiB of HBM per device.

```python
import math
import jax
import jax.numpy as jnp
from jax import lax

D = 2048
K = 10
ROW_DEV = 256
NQ = 1024
CAP = 16
ROWS = 1024


def draw_counts(key):
    shards = ROWS // ROW_DEV
    count_key, hub_key = jax.random.split(jax.random.fold_in(key, 101))
    counts = jax.random.randint(count_key, (shards, shards), CAP // 2, CAP + 1)
    hub = jax.random.randint(hub_key, (), 0, shards)
    source = jnp.arange(shards)[:, None]
    target = jnp.arange(shards)[None, :]
    counts = jnp.where(target == hub, CAP, counts)
    counts = jnp.where((source == shards - 1) & (target == 0), CAP, counts)
    return jnp.where(source == target, 0, counts)


def draw_neighbour(key, part):
    counts = draw_counts(key)
    key = jax.random.fold_in(key, 5)
    side_key, local_key, pick_key = jax.random.split(key, 3)
    shards = ROWS // ROW_DEV
    owner = jnp.arange(ROWS) // ROW_DEV
    column = counts.T[owner]
    inclusive = jnp.cumsum(column, axis=1)
    totals = inclusive[:, -1]
    drawn = jax.random.randint(pick_key, (ROWS, K), 0, 2 ** 30) % totals[:, None]
    source = jnp.sum((inclusive[:, None, :] <= drawn[:, :, None]).astype(jnp.int32), axis=2)
    before = jnp.take_along_axis(inclusive - column, source, axis=1)
    remote = ROW_DEV + source * CAP + drawn - before
    local = jax.random.randint(local_key, (ROWS, K), 0, ROW_DEV)
    side = jax.random.randint(side_key, (ROWS, K), 0, 2)
    picked = jnp.where(side == 0, local, remote)
    picked = picked.at[0, 0].set(ROW_DEV + shards * CAP - 1)
    picked = picked.at[1, 0].set(0)
    return picked.astype(jnp.int32)


def draw_send_rows(key, part):
    key = jax.random.fold_in(key, 7)
    shards = ROWS // ROW_DEV
    keys = jax.random.split(key, shards * shards)
    lists = jax.vmap(lambda item: jax.random.permutation(item, ROW_DEV)[:CAP])(keys)
    return lists.reshape(shards, shards * CAP).astype(jnp.int32)


def draw_gallery(key, part):
    key = jax.random.fold_in(key, 11)
    base_key, row_key, column_key = jax.random.split(key, 3)
    base = jax.random.normal(base_key, (ROWS, D), jnp.float32)
    row_scale = jnp.exp(jax.random.uniform(row_key, (ROWS, 1), jnp.float32, math.log(0.3), math.log(3.0)))
    ramp = jnp.exp(math.log(3.0) * jnp.arange(D, dtype=jnp.float32)[None, :] / D)
    column_scale = 0.5 * ramp * jnp.exp(jax.random.uniform(column_key, (1, D), jnp.float32, -1.15, 1.15))
    return (base * row_scale * column_scale).astype(jnp.bfloat16)


def touch_ends(result, rng, low, top_value):
    longest = result.shape.index(max(result.shape))
    spots = []
    for shift in (0, 1):
        where = [jax.random.randint(jax.random.fold_in(rng, axis), (), 0, length) for axis, length in enumerate(result.shape)]
        where[longest] = (where[longest] + shift) % result.shape[longest]
        spots.append(tuple(where))
    return result.at[spots[0]].set(low).at[spots[1]].set(top_value)


def steps_of(stream_key, extent, cuts, least, top_value):
    loudness = 1.0
    for dim, blocks in cuts:
        heights = jax.random.uniform(jax.random.fold_in(jax.random.fold_in(stream_key, 6), dim), (blocks,), jnp.float32, least / len(cuts), top_value / len(cuts))
        loudness = loudness * jnp.repeat(jnp.exp(heights), extent[dim] // blocks).reshape((-1,) + (1,) * (len(extent) - 1 - dim))
    return loudness


def normal_values(rng, dims, deviation, limit, cuts=(), kind=jnp.bfloat16):
    loudness = steps_of(rng, dims, cuts, -0.22, 0.18) if cuts else 1.0
    values = jax.random.normal(rng, dims, jnp.float32) * deviation * loudness
    return jnp.minimum(jnp.maximum(values, -limit), limit).astype(kind)


def setup_inputs(seed: int = 0, part: int = 0) -> dict:
    key_of = jax.random.split(jax.random.key(seed), 6)
    part_splits = jax.random.split(jax.random.fold_in(key_of[5], part), 6)
    return {
        "gallery": draw_gallery(jax.random.fold_in(jax.random.fold_in(key_of[5], part), 71), part),
        "neighbour": draw_neighbour(jax.random.fold_in(jax.random.fold_in(key_of[5], part), 71), part),
        "weights": touch_ends(jax.random.randint(part_splits[2], (ROWS, K), 1, 5), jax.random.fold_in(part_splits[2], 1), 1, 4).astype(jnp.int32),
        "send_rows": draw_send_rows(jax.random.fold_in(jax.random.fold_in(key_of[5], part), 71), part),
        "queries": normal_values(key_of[4], (NQ, D), 1.0, 6.0, ((0, 4), (1, 4))),
    }


self_weight = 4.0
epsilon = 1e-06

def reference(gallery, neighbour, weights, send_rows, queries):
    shards = ROWS // ROW_DEV
    stacked = gallery.reshape(shards, ROW_DEV, D)

    def refine(operand):
        shard_index, shard_rows, neighbours, weight_rows = operand
        is_local = neighbours < ROW_DEV
        slot_index = jnp.maximum(neighbours - ROW_DEV, 0)
        source = (slot_index // CAP).astype(jnp.int32)
        position = (shard_index * CAP + slot_index % CAP).astype(jnp.int32)
        sent_rows = send_rows[source, position]
        local_index = jnp.minimum(neighbours, ROW_DEV - 1)
        weighted = jnp.zeros((ROW_DEV, D), jnp.float32)
        for which in range(K):
            near_rows = shard_rows[local_index[:, which]].astype(jnp.float32)
            far_rows = stacked[source[:, which], sent_rows[:, which]].astype(jnp.float32)
            picked = jnp.where(is_local[:, which][:, None], near_rows, far_rows)
            weighted = weighted + weight_rows[:, which].astype(jnp.float32)[:, None] * picked
        denominator = self_weight + lax.optimization_barrier(jnp.sum(weight_rows.astype(jnp.float32), axis=1))
        refined = ((self_weight * shard_rows.astype(jnp.float32) + weighted) / denominator[:, None]).astype(jnp.bfloat16)
        floats = refined.astype(jnp.float32)
        inverse = lax.rsqrt(lax.optimization_barrier(jnp.mean(floats * floats, axis=1)) + epsilon) / math.sqrt(D)
        raw = jnp.dot(refined, queries.T, preferred_element_type=jnp.float32)
        return (refined, (raw * inverse[:, None]).astype(jnp.bfloat16))
    refined, scores = lax.map(refine, (jnp.arange(shards, dtype=jnp.int32), stacked, neighbour.reshape(shards, ROW_DEV, K), weights.reshape(shards, ROW_DEV, K)))
    return (refined.reshape(ROWS, D), scores.reshape(ROWS, NQ))
```

```python
import math

import jax
import jax.numpy as jnp
from jax import lax
from jax.sharding import PartitionSpec as P

D = 2048


self_weight = 4.0
epsilon = 1e-06

AXES = ("groups", "gallery", "query")


def weight_matrix(columns, neighbour, weights, width):
    row_count = neighbour.shape[0]
    places = lax.broadcasted_iota(jnp.int32, (row_count, width), 1)
    owners = lax.broadcasted_iota(jnp.int32, (row_count, width), 0)
    matrix = jnp.where(places == owners, jnp.int32(self_weight), 0)
    for which in range(neighbour.shape[1]):
        matrix = matrix + jnp.where(places == columns[:, which][:, None], weights[:, which][:, None], 0)
    return matrix.astype(jnp.bfloat16)


def dot_rows(left, right):
    return lax.dot_general(left, right, (((1,), (1,)), ((), ())), preferred_element_type=jnp.float32)


def generic(gallery, neighbour, weights, send_rows, queries):
    row_count = gallery.shape[0]
    arrived = lax.all_to_all(gallery[send_rows[0]], "gallery", split_axis=0, concat_axis=0, tiled=True)
    table = jnp.concatenate([gallery, arrived], axis=0)
    matrix = weight_matrix(neighbour, neighbour, weights, table.shape[0])
    summed = lax.dot_general(matrix, table, (((1,), (0,)), ((), ())), preferred_element_type=jnp.float32)
    denominator = self_weight + jnp.sum(weights.astype(jnp.float32), axis=1)
    refined = (summed / denominator[:, None]).astype(jnp.bfloat16)
    floats = refined.astype(jnp.float32)
    squares = lax.psum(jnp.sum(floats * floats, axis=1), "query")
    partial_value = dot_rows(refined, lax.all_gather(queries, "gallery", axis=0, tiled=True))
    raw = lax.psum_scatter(partial_value, "query", scatter_dimension=1, tiled=True)
    inverse = lax.rsqrt(squares / D + epsilon) / math.sqrt(D)
    return (refined, (raw * inverse[:, None]).astype(jnp.bfloat16))


def line_of_four(shape, gallery, neighbour, weights, send_rows, queries):
    groups, shards, blocks = shape
    row_count, col_count = gallery.shape
    cap = send_rows.shape[1] // shards
    half_rows = queries.shape[0] // 2
    g, z, q = (lax.axis_index(name) for name in AXES)

    def place(device):
        return (device[0] * shards + device[1]) * blocks + device[2]

    def send(value, to):
        pairs = []
        for gg in range(groups):
            for zz in range(shards):
                for qq in range(blocks):
                    target = to(gg, zz, qq)
                    if target is not None:
                        pairs.append((place((gg, zz, qq)), place(target)))
        return lax.ppermute(value, AXES, pairs)

    def is_far_core(zz, qq):
        return (qq + zz) % 2 == 1

    odd = is_far_core(z, q)
    near = q // 2 == z // 2

    mine = lax.dynamic_slice_in_dim(queries, g * half_rows, half_rows)
    other = lax.dynamic_slice_in_dim(queries, (1 - g) * half_rows, half_rows)
    third = send(mine, lambda g, z, q: (g, z ^ 3, q))
    first = send(mine, lambda g, z, q: (g, z ^ 1, q))

    rows = []
    for step in (1, 2, 3):
        wanted = lax.dynamic_slice_in_dim(send_rows[0], (z ^ step) * cap, cap)
        rows.append(send(gallery[wanted], lambda g, z, q, step=step: (g, z ^ step, q)))
    table = jnp.concatenate([gallery, *rows], axis=0)
    slot = jnp.maximum(neighbour - row_count, 0)
    columns = jnp.where(
        neighbour < row_count, neighbour, row_count + (((slot // cap) ^ z) - 1) * cap + slot % cap
    )
    matrix = weight_matrix(columns, neighbour, weights, table.shape[0])
    summed = lax.dot_general(matrix, table, (((1,), (0,)), ((), ())), preferred_element_type=jnp.float32)
    denominator = self_weight + jnp.sum(weights.astype(jnp.float32), axis=1)
    refined = (summed / denominator[:, None]).astype(jnp.bfloat16)
    refined_pair = send(refined, lambda g, z, q: (g, z, q ^ 1))
    floats = refined.astype(jnp.float32)
    floats_pair = refined_pair.astype(jnp.float32)
    squares = jnp.sum(floats * floats, axis=1) + jnp.sum(floats_pair * floats_pair, axis=1)
    squares = squares + send(squares, lambda g, z, q: (g, z, q ^ 2))
    inverse = lax.rsqrt(squares / D + epsilon) / math.sqrt(D)

    first_other = send(first, lambda g, z, q: (1 - g, z, q))
    leave = jnp.concatenate([jnp.where(odd, mine, first), jnp.where(odd, other, first_other)], axis=0)
    stay = jnp.concatenate([jnp.where(odd, first, mine), jnp.where(odd, first_other, other)], axis=0)
    came = send(leave, lambda g, z, q: (g, z, q ^ 1))
    early = dot_rows(refined, stay) + dot_rows(refined_pair, came)

    a = send(third, lambda g, z, q: (1 - g, z, q) if is_far_core(z, q) else (g, z ^ 1, q ^ 1))
    b = send(third, lambda g, z, q: (g, z ^ 1, q) if is_far_core(z, q) else (1 - g, z, q ^ 1))
    c = send(third, lambda g, z, q: (1 - g, z ^ 1, q) if is_far_core(z, q) else (g, z, q ^ 1))
    d = send(third, lambda g, z, q: None if is_far_core(z, q) else (1 - g, z ^ 1, q ^ 1))
    own = jnp.concatenate([jnp.where(odd, third, b), jnp.where(odd, a, c)], axis=0)
    pair = jnp.concatenate([jnp.where(odd, c, a), jnp.where(odd, b, d)], axis=0)
    late = dot_rows(refined, own) + dot_rows(refined_pair, pair)

    leaving = jnp.where(near, late, early).astype(jnp.bfloat16)
    arriving = send(leaving, lambda g, z, q: (g, z, q ^ 2))
    raw = jnp.where(near, early, late) + arriving.astype(jnp.float32)
    scores = (raw * inverse[:, None]).astype(jnp.bfloat16)
    scores = jnp.where(g == 0, scores, jnp.roll(scores, half_rows, axis=1))
    return (refined, scores)


def solution(mesh):
    shape = tuple(mesh.shape[name] for name in AXES)

    def per_device(*arrays):
        if shape == (2, 4, 4):
            return line_of_four(shape, *arrays)
        return generic(*arrays)

    return jax.shard_map(
        per_device,
        mesh=mesh,
        in_specs=(
            P(("groups", "gallery"), "query"),
            P(("groups", "gallery"), None),
            P(("groups", "gallery"), None),
            P(("groups", "gallery"), None),
            P("gallery", "query"),
        ),
        out_specs=(P(("groups", "gallery"), "query"), P(("groups", "gallery"), "query")),
        check_vma=False,
    )
```

```python
import functools
import math

import jax
import jax.numpy as jnp
from jax import lax
from jax.experimental import pallas as pl
from jax.experimental.pallas import tpu as pltpu
from jax.sharding import PartitionSpec as P

D = 2048


self_weight = 4.0
epsilon = 1e-06

AXES = ("groups", "gallery", "query")


def weight_matrix(columns, neighbour, weights, width):
    row_count = neighbour.shape[0]
    places = lax.broadcasted_iota(jnp.int32, (row_count, width), 1)
    owners = lax.broadcasted_iota(jnp.int32, (row_count, width), 0)
    matrix = jnp.where(places == owners, jnp.int32(self_weight), 0)
    for which in range(neighbour.shape[1]):
        matrix = matrix + jnp.where(places == columns[:, which][:, None], weights[:, which][:, None], 0)
    return matrix.astype(jnp.bfloat16)


def dot_rows(left, right):
    return lax.dot_general(left, right, (((1,), (1,)), ((), ())), preferred_element_type=jnp.float32)


def generic(gallery, neighbour, weights, send_rows, queries):
    row_count = gallery.shape[0]
    arrived = lax.all_to_all(gallery[send_rows[0]], "gallery", split_axis=0, concat_axis=0, tiled=True)
    table = jnp.concatenate([gallery, arrived], axis=0)
    matrix = weight_matrix(neighbour, neighbour, weights, table.shape[0])
    summed = lax.dot_general(matrix, table, (((1,), (0,)), ((), ())), preferred_element_type=jnp.float32)
    denominator = self_weight + jnp.sum(weights.astype(jnp.float32), axis=1)
    refined = (summed / denominator[:, None]).astype(jnp.bfloat16)
    floats = refined.astype(jnp.float32)
    squares = lax.psum(jnp.sum(floats * floats, axis=1), "query")
    partial_value = dot_rows(refined, lax.all_gather(queries, "gallery", axis=0, tiled=True))
    raw = lax.psum_scatter(partial_value, "query", scatter_dimension=1, tiled=True)
    inverse = lax.rsqrt(squares / D + epsilon) / math.sqrt(D)
    return (refined, (raw * inverse[:, None]).astype(jnp.bfloat16))


VMEM = pl.BlockSpec(memory_space=pltpu.VMEM)
SPARE = 16


def call(kernel, outs, *operands, scratch=(), flops=0, specs=None):
    size = sum(math.prod(item.shape) * item.dtype.itemsize for item in (*outs, *operands))
    return pl.pallas_call(
        kernel,
        out_shape=list(outs),
        in_specs=specs or [VMEM] * len(operands),
        out_specs=[VMEM] * len(outs),
        scratch_shapes=list(scratch),
        compiler_params=pltpu.CompilerParams(vmem_limit_bytes=16 * 1024 * 1024),
        cost_estimate=pl.CostEstimate(flops=flops, bytes_accessed=size, transcendentals=0),
    )(*operands)


def array(shape, kind):
    return pltpu.VMEM(shape, kind)


def dot_columns(left, right):
    return lax.dot_general(left, right, (((0,), (0,)), ((), ())), preferred_element_type=jnp.float32)


def three_parts(row):
    high = row.astype(jnp.bfloat16).astype(jnp.float32)
    middle = (row - high).astype(jnp.bfloat16).astype(jnp.float32)
    low = row - high - middle
    index = lax.broadcasted_iota(jnp.int32, row.shape, 0)
    parts = jnp.where(index == 0, high, jnp.where(index == 1, middle, jnp.where(index == 2, low, 0.0)))
    return parts.astype(jnp.bfloat16)


def pack_kernel(
    cap, queries, gallery, send_rows, to_third, to_first, to_second, rows_in, lists_in, picked, arrived
):
    g, z = lax.axis_index("groups"), lax.axis_index("gallery")
    half = to_third.shape[0] - cap
    mine = queries.at[pl.ds(pl.multiple_of(g * half, half), half), :]
    copies = [
        pltpu.make_async_copy(send_rows, lists_in, arrived.at[0]),
        pltpu.make_async_copy(gallery, rows_in, arrived.at[1]),
        pltpu.make_async_copy(mine, to_third.at[0:half, :], arrived.at[2]),
        pltpu.make_async_copy(mine, to_first.at[0:half, :], arrived.at[3]),
    ]
    for copy in copies:
        copy.start()
    copies[0].wait()
    shape = (rows_in.shape[0], lists_in.shape[1])
    hot = jnp.where(lax.broadcasted_iota(jnp.int32, shape, 0) == lists_in[0:1, :], 1.0, 0.0).astype(jnp.bfloat16)
    copies[1].wait()
    picked[...] = dot_columns(hot, rows_in[...]).astype(jnp.bfloat16)

    def rows(step):
        return picked[pl.ds(pl.multiple_of(jnp.bitwise_xor(z, step) * cap, cap), cap), :]

    to_third[half:, :] = rows(3)
    to_first[half:, :] = rows(1)
    to_second[...] = rows(2)
    copies[2].wait()
    copies[3].wait()


def refine_kernel(cap, gallery, neighbour, weights, first, second, third, refined, squares):
    z = lax.axis_index("gallery")
    row_count, col_count = gallery.shape
    index = neighbour[...]
    weight = weights[...].astype(jnp.float32)
    slot = jnp.maximum(index - row_count, 0)
    far = (jnp.bitwise_xor(lax.div(slot, cap), z) - 1) * cap + lax.rem(slot, cap)
    far = jnp.where(index >= row_count, far, -1)

    def matrix(places, height, base):
        places_of = lax.broadcasted_iota(jnp.int32, (height, row_count), 0)
        total = base(places_of)
        for which in range(index.shape[0]):
            total = total + jnp.where(places_of == places[which : which + 1, :], weight[which : which + 1, :], 0.0)
        return total.astype(jnp.bfloat16)

    def own(places_of):
        return jnp.where(places_of == lax.broadcasted_iota(jnp.int32, places_of.shape, 1), self_weight, 0.0)

    near_matrix = matrix(index, row_count, own)
    far_matrix = matrix(far, 3 * cap, lambda places_of: jnp.zeros(places_of.shape, jnp.float32))
    half = first.shape[0] - cap
    table = jnp.concatenate([first[half:, :], second[...], third[half:, :]], axis=0)
    summed = dot_columns(near_matrix, gallery[...]) + dot_columns(far_matrix, table)
    denominator = dot_columns(near_matrix, jnp.ones((row_count, 128), jnp.bfloat16)) + dot_columns(
        far_matrix, jnp.ones((3 * cap, 128), jnp.bfloat16)
    )
    for start in range(0, col_count, 128):
        refined[:, start : start + 128] = (summed[:, start : start + 128] / denominator).astype(jnp.bfloat16)
    floats = refined[...].astype(jnp.float32)
    floats = floats * floats
    high = floats.astype(jnp.bfloat16)
    low = (floats - high.astype(jnp.float32)).astype(jnp.bfloat16)
    ones = jnp.ones((SPARE, col_count), jnp.bfloat16)
    squares[...] = dot_rows(ones, high) + dot_rows(ones, low)


def early_kernel(refined, squares, queries, first, first_other, keep, give):
    g, z, q = (lax.axis_index(name) for name in AXES)
    half = first_other.shape[0]
    row_count = refined.shape[0]
    odd = lax.rem(q + z, 2) == 1
    rows = refined[...]
    for place, one in ((g, first), (1 - g, first_other)):
        columns = pl.ds(pl.multiple_of(place * half, half), half)
        mine = queries[columns, :]
        came = one[0:half, :]
        keep[:, columns] = dot_rows(rows, jnp.where(odd, came, mine))
        give[0:row_count, columns] = dot_rows(rows, jnp.where(odd, mine, came)).astype(jnp.bfloat16)
    give[row_count:, :] = three_parts(squares[...])


def late_kernel(refined, third, third_other, second, second_other, keep, give):
    g, z, q = (lax.axis_index(name) for name in AXES)
    half = third_other.shape[0]
    odd = lax.rem(q + z, 2) == 1
    rows = refined[...]
    for place, one, two in ((g, third, second), (1 - g, third_other, second_other)):
        columns = pl.ds(pl.multiple_of(place * half, half), half)
        one, two = one[0:half, :], two[0:half, :]
        keep[:, columns] = dot_rows(rows, jnp.where(odd, one, two))
        give[:, columns] = dot_rows(rows, jnp.where(odd, two, one)).astype(jnp.bfloat16)


def whole(parts):
    return jnp.sum(parts.astype(jnp.float32), axis=0, keepdims=True)


def leave_kernel(early, early_came, squares, late, late_came, stay, leave):
    z, q = lax.axis_index("gallery"), lax.axis_index("query")
    row_count = late.shape[0]
    near = lax.div(q, 2) == lax.div(z, 2)
    early_sum = early[...] + early_came[0:row_count, :].astype(jnp.float32)
    late_sum = late[...] + late_came[...].astype(jnp.float32)
    row = squares[...] + whole(early_came[row_count:, :])
    stay[0:row_count, :] = jnp.where(near, early_sum, late_sum)
    stay[row_count:, :] = row
    leave[0:row_count, :] = jnp.where(near, late_sum, early_sum).astype(jnp.bfloat16)
    leave[row_count:, :] = three_parts(row)


def score_kernel(stay, came, scores):
    row_count = scores.shape[0]
    squares = stay[row_count : row_count + 1, :] + whole(came[row_count:, :])
    inverse = lax.rsqrt(squares / D + epsilon) / math.sqrt(D)
    shape = (row_count, row_count)
    same = lax.broadcasted_iota(jnp.int32, shape, 0) == lax.broadcasted_iota(jnp.int32, shape, 1)
    inverse = jnp.sum(jnp.where(same, inverse, 0.0), axis=1, keepdims=True)
    scores[...] = ((stay[0:row_count, :] + came[0:row_count, :].astype(jnp.float32)) * inverse).astype(jnp.bfloat16)


def line_of_four(shape, gallery, neighbour, weights, send_rows, queries):
    groups, shards, blocks = shape
    row_count, col_count = gallery.shape
    query_count = queries.shape[0]
    half = query_count // 2
    cap = send_rows.shape[1] // shards
    low, high = jnp.bfloat16, jnp.float32

    def place(device):
        return (device[0] * shards + device[1]) * blocks + device[2]

    def send(value, to):
        pairs = []
        for g in range(groups):
            for z in range(shards):
                for q in range(blocks):
                    pairs.append((place((g, z, q)), place(to(g, z, q))))
        return lax.ppermute(value, AXES, pairs)

    to_third, to_first, to_second = call(
        functools.partial(pack_kernel, cap),
        [array((half + cap, col_count), low), array((half + cap, col_count), low), array((cap, col_count), low)],
        *(pltpu.with_memory_space_constraint(item, pltpu.HBM) for item in (queries, gallery, send_rows)),
        specs=[pl.BlockSpec(memory_space=pltpu.HBM)] * 3,
        scratch=[
            pltpu.VMEM(gallery.shape, low),
            pltpu.VMEM(send_rows.shape, jnp.int32),
            pltpu.VMEM((shards * cap, col_count), low),
            pltpu.SemaphoreType.DMA((4,)),
        ],
    )
    third = send(to_third, lambda g, z, q: (g, z ^ 3, q))
    first = send(to_first, lambda g, z, q: (g, z ^ 1, q))
    second_rows = send(to_second, lambda g, z, q: (g, z ^ 2, q))

    passed, second_rows = lax.optimization_barrier((third[0:half], second_rows))
    third_other = send(passed, lambda g, z, q: (1 - g, z, q))
    second = send(passed, lambda g, z, q: (g, z ^ 1, q))
    second_other = send(passed, lambda g, z, q: (1 - g, z ^ 1, q))
    first_other = send(first[0:half], lambda g, z, q: (1 - g, z, q))

    refined, squares = call(
        functools.partial(refine_kernel, cap),
        [array((row_count, col_count), low), array((SPARE, row_count), high)],
        gallery,
        neighbour.T,
        weights.T,
        first,
        second_rows,
        third,
    )
    early, early_give = call(
        early_kernel,
        [array((row_count, query_count), high), array((row_count + SPARE, query_count), low)],
        refined,
        squares,
        queries,
        first,
        first_other,
    )
    early_came = send(early_give, lambda g, z, q: (g, z, q ^ 1))
    late, late_give = call(
        late_kernel,
        [array((row_count, query_count), high), array((row_count, query_count), low)],
        refined,
        third,
        third_other,
        second,
        second_other,
    )
    late_came = send(late_give, lambda g, z, q: (g, z, q ^ 1))
    stay, leave = call(
        leave_kernel,
        [array((row_count + SPARE, query_count), high), array((row_count + SPARE, query_count), low)],
        early,
        early_came,
        squares,
        late,
        late_came,
    )
    came = send(leave, lambda g, z, q: (g, z, q ^ 2))
    (scores,) = call(score_kernel, [jax.ShapeDtypeStruct((row_count, query_count), low)], stay, came)
    return (refined, scores)


def solution(mesh):
    shape = tuple(mesh.shape[name] for name in AXES)

    def per_device(*arrays):
        if shape == (2, 4, 4):
            return line_of_four(shape, *arrays)
        return generic(*arrays)

    return jax.shard_map(
        per_device,
        mesh=mesh,
        in_specs=(
            P(("groups", "gallery"), "query"),
            P(("groups", "gallery"), None),
            P(("groups", "gallery"), None),
            P(("groups", "gallery"), None),
            P("gallery", "query"),
        ),
        out_specs=(P(("groups", "gallery"), "query"), P(("groups", "gallery"), "query")),
        check_vma=False,
    )
```

```python
import functools
import math

import jax
import jax.numpy as jnp
from jax import lax
from jax.experimental import pallas as pl
from jax.experimental.pallas import tpu as pltpu
from jax.sharding import PartitionSpec as P

D = 2048


self_weight = 4.0
epsilon = 1e-06

AXES = ("groups", "gallery", "query")


def weight_matrix(columns, neighbour, weights, width):
    row_count = neighbour.shape[0]
    places = lax.broadcasted_iota(jnp.int32, (row_count, width), 1)
    owners = lax.broadcasted_iota(jnp.int32, (row_count, width), 0)
    matrix = jnp.where(places == owners, jnp.int32(self_weight), 0)
    for which in range(neighbour.shape[1]):
        matrix = matrix + jnp.where(places == columns[:, which][:, None], weights[:, which][:, None], 0)
    return matrix.astype(jnp.bfloat16)


def dot_rows(left, right):
    return lax.dot_general(left, right, (((1,), (1,)), ((), ())), preferred_element_type=jnp.float32)


def generic(gallery, neighbour, weights, send_rows, queries):
    row_count = gallery.shape[0]
    arrived = lax.all_to_all(gallery[send_rows[0]], "gallery", split_axis=0, concat_axis=0, tiled=True)
    table = jnp.concatenate([gallery, arrived], axis=0)
    matrix = weight_matrix(neighbour, neighbour, weights, table.shape[0])
    summed = lax.dot_general(matrix, table, (((1,), (0,)), ((), ())), preferred_element_type=jnp.float32)
    denominator = self_weight + jnp.sum(weights.astype(jnp.float32), axis=1)
    refined = (summed / denominator[:, None]).astype(jnp.bfloat16)
    floats = refined.astype(jnp.float32)
    squares = lax.psum(jnp.sum(floats * floats, axis=1), "query")
    partial_value = dot_rows(refined, lax.all_gather(queries, "gallery", axis=0, tiled=True))
    raw = lax.psum_scatter(partial_value, "query", scatter_dimension=1, tiled=True)
    inverse = lax.rsqrt(squares / D + epsilon) / math.sqrt(D)
    return (refined, (raw * inverse[:, None]).astype(jnp.bfloat16))


VMEM = pl.BlockSpec(memory_space=pltpu.VMEM)
SPARE = 16


def call(kernel, outs, *operands, scratch=(), flops=0, specs=None):
    size = sum(math.prod(item.shape) * item.dtype.itemsize for item in (*outs, *operands))
    return pl.pallas_call(
        kernel,
        out_shape=list(outs),
        in_specs=specs or [VMEM] * len(operands),
        out_specs=[VMEM] * len(outs),
        scratch_shapes=list(scratch),
        compiler_params=pltpu.CompilerParams(vmem_limit_bytes=16 * 1024 * 1024),
        cost_estimate=pl.CostEstimate(flops=flops, bytes_accessed=size, transcendentals=0),
    )(*operands)


def array(shape, kind):
    return pltpu.VMEM(shape, kind)


def dot_columns(left, right):
    return lax.dot_general(left, right, (((0,), (0,)), ((), ())), preferred_element_type=jnp.float32)


def three_parts(row):
    high = row.astype(jnp.bfloat16).astype(jnp.float32)
    middle = (row - high).astype(jnp.bfloat16).astype(jnp.float32)
    low = row - high - middle
    index = lax.broadcasted_iota(jnp.int32, row.shape, 0)
    parts = jnp.where(index == 0, high, jnp.where(index == 1, middle, jnp.where(index == 2, low, 0.0)))
    return parts.astype(jnp.bfloat16)


def pack_kernel(
    cap, queries, gallery, send_rows, to_third, to_first, to_second, rows_in, lists_in, picked, arrived
):
    g, z = lax.axis_index("groups"), lax.axis_index("gallery")
    half = to_third.shape[0] - cap
    mine = queries.at[pl.ds(pl.multiple_of(g * half, half), half), :]
    copies = [
        pltpu.make_async_copy(send_rows, lists_in, arrived.at[0]),
        pltpu.make_async_copy(gallery, rows_in, arrived.at[1]),
        pltpu.make_async_copy(mine, to_third.at[0:half, :], arrived.at[2]),
        pltpu.make_async_copy(mine, to_first.at[0:half, :], arrived.at[3]),
    ]
    for copy in copies:
        copy.start()
    copies[0].wait()
    shape = (rows_in.shape[0], lists_in.shape[1])
    hot = jnp.where(lax.broadcasted_iota(jnp.int32, shape, 0) == lists_in[0:1, :], 1.0, 0.0).astype(jnp.bfloat16)
    copies[1].wait()
    picked[...] = dot_columns(hot, rows_in[...]).astype(jnp.bfloat16)

    def rows(step):
        return picked[pl.ds(pl.multiple_of(jnp.bitwise_xor(z, step) * cap, cap), cap), :]

    to_third[half:, :] = rows(3)
    to_first[half:, :] = rows(1)
    to_second[...] = rows(2)
    copies[2].wait()
    copies[3].wait()


def near_kernel(cap, gallery, neighbour, weights, summed, denominator, far_matrix):
    z = lax.axis_index("gallery")
    row_count = gallery.shape[0]
    index = neighbour[...]
    weight = weights[...].astype(jnp.float32)
    slot = jnp.maximum(index - row_count, 0)
    far = (jnp.bitwise_xor(lax.div(slot, cap), z) - 1) * cap + lax.rem(slot, cap)
    far = jnp.where(index >= row_count, far, -1)

    def matrix(places, height, base):
        places_of = lax.broadcasted_iota(jnp.int32, (height, row_count), 0)
        total = base(places_of)
        for which in range(index.shape[0]):
            total = total + jnp.where(places_of == places[which : which + 1, :], weight[which : which + 1, :], 0.0)
        return total.astype(jnp.bfloat16)

    def own(places_of):
        return jnp.where(places_of == lax.broadcasted_iota(jnp.int32, places_of.shape, 1), self_weight, 0.0)

    near_matrix = matrix(index, row_count, own)
    far_matrix[...] = matrix(far, 3 * cap, lambda places_of: jnp.zeros(places_of.shape, jnp.float32))
    summed[...] = dot_columns(near_matrix, gallery[...])
    denominator[...] = dot_columns(near_matrix, jnp.ones((row_count, 128), jnp.bfloat16)) + dot_columns(
        far_matrix[...], jnp.ones((3 * cap, 128), jnp.bfloat16)
    )


def refine_kernel(cap, summed, denominator, far_matrix, first, second, third, refined, squares):
    row_count, col_count = summed.shape
    half = first.shape[0] - cap
    table = jnp.concatenate([first[half:, :], second[...], third[half:, :]], axis=0)
    total = summed[...] + dot_columns(far_matrix[...], table)
    for start in range(0, col_count, 128):
        refined[:, start : start + 128] = (total[:, start : start + 128] / denominator[...]).astype(jnp.bfloat16)
    floats = refined[...].astype(jnp.float32)
    floats = floats * floats
    high = floats.astype(jnp.bfloat16)
    low = (floats - high.astype(jnp.float32)).astype(jnp.bfloat16)
    ones = jnp.ones((SPARE, col_count), jnp.bfloat16)
    squares[...] = dot_rows(ones, high) + dot_rows(ones, low)


def early_kernel(refined, squares, queries, first, first_other, keep, give):
    g, z, q = (lax.axis_index(name) for name in AXES)
    half = queries.shape[0] // 2
    row_count = refined.shape[0]
    odd = lax.rem(q + z, 2) == 1
    rows = refined[...]
    for place, one in ((g, first), (1 - g, first_other)):
        columns = pl.ds(pl.multiple_of(place * half, half), half)
        mine = queries[columns, :]
        came = one[0:half, :]
        keep[:, columns] = dot_rows(rows, jnp.where(odd, came, mine))
        give[0:row_count, columns] = dot_rows(rows, jnp.where(odd, mine, came)).astype(jnp.bfloat16)
    give[row_count:, :] = three_parts(squares[...])


def late_kernel(refined, refined_pair, own_odd, own_even, pair_odd, pair_even, partial):
    z, q = lax.axis_index("gallery"), lax.axis_index("query")
    half = partial.shape[1]
    odd = lax.rem(q + z, 2) == 1
    own = jnp.where(odd, own_odd[0:half, :], own_even[0:half, :])
    pair = jnp.where(odd, pair_odd[0:half, :], pair_even[0:half, :])
    partial[...] = dot_rows(refined[...], own) + dot_rows(refined_pair[...], pair)


def whole(parts):
    return jnp.sum(parts.astype(jnp.float32), axis=0, keepdims=True)


def first_half():
    g, z, q = (lax.axis_index(name) for name in AXES)
    odd = lax.rem(q + z, 2) == 1
    return jnp.where(odd, 1 - g, g), lax.div(q, 2) == lax.div(z, 2)


def leave_most_kernel(early, early_came, squares, late, early_sum, stay, chip_squares, leave):
    row_count, half = late.shape
    place, near = first_half()
    early_sum[...] = early[...] + early_came[0:row_count, :].astype(jnp.float32)
    near_part = early_sum[:, pl.ds(pl.multiple_of(place * half, half), half)]
    row = squares[...] + whole(early_came[row_count:, :])
    parts = three_parts(row)
    chip_squares[...] = row
    stay[...] = jnp.where(near, near_part, late[...])
    leave[0:row_count, :] = jnp.where(near, late[...], near_part).astype(jnp.bfloat16)
    leave[row_count : row_count + SPARE, :] = parts[:, 0:half]
    leave[row_count + SPARE :, :] = parts[:, half:]


def leave_last_kernel(early_sum, late, stay, leave):
    half = late.shape[1]
    place, near = first_half()
    near_part = early_sum[:, pl.ds(pl.multiple_of((1 - place) * half, half), half)]
    stay[...] = jnp.where(near, near_part, late[...])
    leave[...] = jnp.where(near, late[...], near_part).astype(jnp.bfloat16)


def score_kernel(stay_most, chip_squares, came_most, stay_last, came_last, scores):
    row_count, half = stay_most.shape
    place, _ = first_half()
    there = (whole(came_most[row_count : row_count + SPARE, :]), whole(came_most[row_count + SPARE :, :]))
    squares = chip_squares[0:1, :] + jnp.concatenate(there, axis=1)
    inverse = lax.rsqrt(squares / D + epsilon) / math.sqrt(D)
    shape = (row_count, row_count)
    same = lax.broadcasted_iota(jnp.int32, shape, 0) == lax.broadcasted_iota(jnp.int32, shape, 1)
    inverse = jnp.sum(jnp.where(same, inverse, 0.0), axis=1, keepdims=True)
    for where, stay, came in ((place, stay_most, came_most), (1 - place, stay_last, came_last)):
        raw = stay[...] + came[0:row_count, :].astype(jnp.float32)
        scores[:, pl.ds(pl.multiple_of(where * half, half), half)] = (raw * inverse).astype(jnp.bfloat16)


def line_of_four(shape, gallery, neighbour, weights, send_rows, queries):
    groups, shards, blocks = shape
    row_count, col_count = gallery.shape
    query_count = queries.shape[0]
    half = query_count // 2
    cap = send_rows.shape[1] // shards
    low, high = jnp.bfloat16, jnp.float32

    def place(device):
        return (device[0] * shards + device[1]) * blocks + device[2]

    def send(value, to, only=lambda g, z, q: True):
        pairs = []
        for g in range(groups):
            for z in range(shards):
                for q in range(blocks):
                    if only(g, z, q):
                        pairs.append((place((g, z, q)), place(to(g, z, q))))
        return lax.ppermute(value, AXES, pairs)

    def is_odd(z, q):
        return (q + z) % 2 == 1

    to_third, to_first, to_second = call(
        functools.partial(pack_kernel, cap),
        [array((half + cap, col_count), low), array((half + cap, col_count), low), array((cap, col_count), low)],
        *(pltpu.with_memory_space_constraint(item, pltpu.HBM) for item in (queries, gallery, send_rows)),
        specs=[pl.BlockSpec(memory_space=pltpu.HBM)] * 3,
        scratch=[
            pltpu.VMEM(gallery.shape, low),
            pltpu.VMEM(send_rows.shape, jnp.int32),
            pltpu.VMEM((shards * cap, col_count), low),
            pltpu.SemaphoreType.DMA((4,)),
        ],
    )
    third = send(to_third, lambda g, z, q: (g, z ^ 3, q))
    first = send(to_first, lambda g, z, q: (g, z ^ 1, q))
    second_rows = send(to_second, lambda g, z, q: (g, z ^ 2, q))

    first_other = send(first, lambda g, z, q: (1 - g, z, q))
    summed, denominator, far_matrix = call(
        functools.partial(near_kernel, cap),
        [
            array((row_count, col_count), high),
            array((row_count, 128), high),
            array(((shards - 1) * cap, row_count), low),
        ],
        gallery,
        neighbour.T,
        weights.T,
    )
    passed, second_rows, summed = lax.optimization_barrier((third, second_rows, summed))
    a = send(passed, lambda g, z, q: (1 - g, z, q) if is_odd(z, q) else (g, z ^ 1, q ^ 1))
    b = send(passed, lambda g, z, q: (g, z ^ 1, q) if is_odd(z, q) else (1 - g, z, q ^ 1))
    c = send(passed, lambda g, z, q: (1 - g, z ^ 1, q) if is_odd(z, q) else (g, z, q ^ 1))
    d = send(passed, lambda g, z, q: (1 - g, z, q) if is_odd(z, q) else (1 - g, z ^ 1, q ^ 1))

    refined, squares = call(
        functools.partial(refine_kernel, cap),
        [array((row_count, col_count), low), array((SPARE, row_count), high)],
        summed,
        denominator,
        far_matrix,
        first,
        second_rows,
        third,
    )
    refined_pair = send(refined, lambda g, z, q: (g, z, q ^ 1))
    early, early_give = call(
        early_kernel,
        [array((row_count, query_count), high), array((row_count + SPARE, query_count), low)],
        refined,
        squares,
        queries,
        first,
        first_other,
    )
    early_came = send(early_give, lambda g, z, q: (g, z, q ^ 1))

    (late_most,) = call(late_kernel, [array((row_count, half), high)], refined, refined_pair, a, b, b, a)
    early_sum, stay_most, chip_squares, leave = call(
        leave_most_kernel,
        [
            array((row_count, query_count), high),
            array((row_count, half), high),
            array((SPARE, row_count), high),
            array((row_count + 2 * SPARE, half), low),
        ],
        early,
        early_came,
        squares,
        late_most,
    )
    came_most = send(leave, lambda g, z, q: (g, z, q ^ 2))

    c, d, _ = lax.optimization_barrier((c, d, leave))
    (late_last,) = call(late_kernel, [array((row_count, half), high)], refined, refined_pair, third, c, c, d)
    stay_last, leave = call(
        leave_last_kernel, [array((row_count, half), high), array((row_count, half), low)], early_sum, late_last
    )
    came_last = send(leave, lambda g, z, q: (g, z, q ^ 2))
    (scores,) = call(
        score_kernel,
        [jax.ShapeDtypeStruct((row_count, query_count), low)],
        stay_most,
        chip_squares,
        came_most,
        stay_last,
        came_last,
    )
    return (refined, scores)


def solution(mesh):
    shape = tuple(mesh.shape[name] for name in AXES)

    def per_device(*arrays):
        if shape == (2, 4, 4):
            return line_of_four(shape, *arrays)
        return generic(*arrays)

    return jax.shard_map(
        per_device,
        mesh=mesh,
        in_specs=(
            P(("groups", "gallery"), "query"),
            P(("groups", "gallery"), None),
            P(("groups", "gallery"), None),
            P(("groups", "gallery"), None),
            P("gallery", "query"),
        ),
        out_specs=(P(("groups", "gallery"), "query"), P(("groups", "gallery"), "query")),
        check_vma=False,
    )
```

```python
import functools
import math

import jax
import jax.numpy as jnp
from jax import lax
from jax.experimental import pallas as pl
from jax.experimental.pallas import tpu as pltpu
from jax.sharding import PartitionSpec as P

D = 2048


self_weight = 4.0
epsilon = 1e-06

AXES = ("groups", "gallery", "query")


def weight_matrix(columns, neighbour, weights, width):
    row_count = neighbour.shape[0]
    places = lax.broadcasted_iota(jnp.int32, (row_count, width), 1)
    owners = lax.broadcasted_iota(jnp.int32, (row_count, width), 0)
    matrix = jnp.where(places == owners, jnp.int32(self_weight), 0)
    for which in range(neighbour.shape[1]):
        matrix = matrix + jnp.where(places == columns[:, which][:, None], weights[:, which][:, None], 0)
    return matrix.astype(jnp.bfloat16)


def dot_rows(left, right):
    return lax.dot_general(left, right, (((1,), (1,)), ((), ())), preferred_element_type=jnp.float32)


def generic(gallery, neighbour, weights, send_rows, queries):
    row_count = gallery.shape[0]
    arrived = lax.all_to_all(gallery[send_rows[0]], "gallery", split_axis=0, concat_axis=0, tiled=True)
    table = jnp.concatenate([gallery, arrived], axis=0)
    matrix = weight_matrix(neighbour, neighbour, weights, table.shape[0])
    summed = lax.dot_general(matrix, table, (((1,), (0,)), ((), ())), preferred_element_type=jnp.float32)
    denominator = self_weight + jnp.sum(weights.astype(jnp.float32), axis=1)
    refined = (summed / denominator[:, None]).astype(jnp.bfloat16)
    floats = refined.astype(jnp.float32)
    squares = lax.psum(jnp.sum(floats * floats, axis=1), "query")
    partial_value = dot_rows(refined, lax.all_gather(queries, "gallery", axis=0, tiled=True))
    raw = lax.psum_scatter(partial_value, "query", scatter_dimension=1, tiled=True)
    inverse = lax.rsqrt(squares / D + epsilon) / math.sqrt(D)
    return (refined, (raw * inverse[:, None]).astype(jnp.bfloat16))


VMEM = pl.BlockSpec(memory_space=pltpu.VMEM)
SPARE = 16


def call(kernel, outs, *operands, scratch=(), flops=0, specs=None):
    size = sum(math.prod(item.shape) * item.dtype.itemsize for item in (*outs, *operands))
    return pl.pallas_call(
        kernel,
        out_shape=list(outs),
        in_specs=specs or [VMEM] * len(operands),
        out_specs=[VMEM] * len(outs),
        scratch_shapes=list(scratch),
        compiler_params=pltpu.CompilerParams(vmem_limit_bytes=16 * 1024 * 1024),
        cost_estimate=pl.CostEstimate(flops=flops, bytes_accessed=size, transcendentals=0),
    )(*operands)


def array(shape, kind):
    return pltpu.VMEM(shape, kind)


def dot_columns(left, right):
    return lax.dot_general(left, right, (((0,), (0,)), ((), ())), preferred_element_type=jnp.float32)


def three_parts(row):
    high = row.astype(jnp.bfloat16).astype(jnp.float32)
    middle = (row - high).astype(jnp.bfloat16).astype(jnp.float32)
    low = row - high - middle
    index = lax.broadcasted_iota(jnp.int32, row.shape, 0)
    parts = jnp.where(index == 0, high, jnp.where(index == 1, middle, jnp.where(index == 2, low, 0.0)))
    return parts.astype(jnp.bfloat16)


def pack_kernel(
    cap, queries, gallery, send_rows, to_third, to_first, to_second, rows_in, lists_in, picked, arrived
):
    g, z = lax.axis_index("groups"), lax.axis_index("gallery")
    half = to_third.shape[0] - cap
    mine = queries.at[pl.ds(pl.multiple_of(g * half, half), half), :]
    copies = [
        pltpu.make_async_copy(send_rows, lists_in, arrived.at[0]),
        pltpu.make_async_copy(gallery, rows_in, arrived.at[1]),
        pltpu.make_async_copy(mine, to_third.at[0:half, :], arrived.at[2]),
        pltpu.make_async_copy(mine, to_first.at[0:half, :], arrived.at[3]),
    ]
    for copy in copies:
        copy.start()
    copies[0].wait()
    shape = (rows_in.shape[0], lists_in.shape[1])
    hot = jnp.where(lax.broadcasted_iota(jnp.int32, shape, 0) == lists_in[0:1, :], 1.0, 0.0).astype(jnp.bfloat16)
    copies[1].wait()
    picked[...] = dot_columns(hot, rows_in[...]).astype(jnp.bfloat16)

    def rows(step):
        return picked[pl.ds(pl.multiple_of(jnp.bitwise_xor(z, step) * cap, cap), cap), :]

    to_third[half:, :] = rows(3)
    to_first[half:, :] = rows(1)
    to_second[...] = rows(2)
    copies[2].wait()
    copies[3].wait()


def refine_kernel(cap, gallery, neighbour, weights, first, second, third, refined, squares):
    z = lax.axis_index("gallery")
    row_count, col_count = gallery.shape
    index = neighbour[...]
    weight = weights[...].astype(jnp.float32)
    slot = jnp.maximum(index - row_count, 0)
    far = (jnp.bitwise_xor(lax.div(slot, cap), z) - 1) * cap + lax.rem(slot, cap)
    far = jnp.where(index >= row_count, far, -1)

    def matrix(places, height, base):
        places_of = lax.broadcasted_iota(jnp.int32, (height, row_count), 0)
        total = base(places_of)
        for which in range(index.shape[0]):
            total = total + jnp.where(places_of == places[which : which + 1, :], weight[which : which + 1, :], 0.0)
        return total.astype(jnp.bfloat16)

    def own(places_of):
        return jnp.where(places_of == lax.broadcasted_iota(jnp.int32, places_of.shape, 1), self_weight, 0.0)

    near_matrix = matrix(index, row_count, own)
    far_matrix = matrix(far, 3 * cap, lambda places_of: jnp.zeros(places_of.shape, jnp.float32))
    half = first.shape[0] - cap
    table = jnp.concatenate([first[half:, :], second[...], third[half:, :]], axis=0)
    summed = dot_columns(near_matrix, gallery[...]) + dot_columns(far_matrix, table)
    denominator = dot_columns(near_matrix, jnp.ones((row_count, 128), jnp.bfloat16)) + dot_columns(
        far_matrix, jnp.ones((3 * cap, 128), jnp.bfloat16)
    )
    for start in range(0, col_count, 128):
        refined[:, start : start + 128] = (summed[:, start : start + 128] / denominator).astype(jnp.bfloat16)
    floats = refined[...].astype(jnp.float32)
    floats = floats * floats
    high = floats.astype(jnp.bfloat16)
    low = (floats - high.astype(jnp.float32)).astype(jnp.bfloat16)
    ones = jnp.ones((SPARE, col_count), jnp.bfloat16)
    squares[...] = dot_rows(ones, high) + dot_rows(ones, low)


def early_kernel(refined, squares, queries, first, first_other, keep, give):
    g, z, q = (lax.axis_index(name) for name in AXES)
    half = first_other.shape[0]
    row_count = refined.shape[0]
    odd = lax.rem(q + z, 2) == 1
    rows = refined[...]
    for place, one in ((g, first), (1 - g, first_other)):
        columns = pl.ds(pl.multiple_of(place * half, half), half)
        mine = queries[columns, :]
        came = one[0:half, :]
        keep[:, columns] = dot_rows(rows, jnp.where(odd, came, mine))
        give[0:row_count, columns] = dot_rows(rows, jnp.where(odd, mine, came)).astype(jnp.bfloat16)
    give[row_count:, :] = three_parts(squares[...])


def late_kernel(refined, third, second_other, third_other, second, keep, give):
    g, z, q = (lax.axis_index(name) for name in AXES)
    half = third_other.shape[0]
    odd = lax.rem(q + z, 2) == 1
    rows = refined[...]
    for place, one, two in ((g, third, second), (1 - g, third_other, second_other)):
        columns = pl.ds(pl.multiple_of(place * half, half), half)
        one, two = one[0:half, :], two[0:half, :]
        keep[:, columns] = dot_rows(rows, jnp.where(odd, one, two))
        give[:, columns] = dot_rows(rows, jnp.where(odd, two, one)).astype(jnp.bfloat16)


def whole(parts):
    return jnp.sum(parts.astype(jnp.float32), axis=0, keepdims=True)


def leave_kernel(early, early_came, squares, late, late_came, stay, leave):
    z, q = lax.axis_index("gallery"), lax.axis_index("query")
    row_count = late.shape[0]
    near = lax.div(q, 2) == lax.div(z, 2)
    early_sum = early[...] + early_came[0:row_count, :].astype(jnp.float32)
    late_sum = late[...] + late_came[...].astype(jnp.float32)
    row = squares[...] + whole(early_came[row_count:, :])
    stay[0:row_count, :] = jnp.where(near, early_sum, late_sum)
    stay[row_count:, :] = row
    leave[0:row_count, :] = jnp.where(near, late_sum, early_sum).astype(jnp.bfloat16)
    leave[row_count:, :] = three_parts(row)


def score_kernel(stay, came, scores):
    row_count = scores.shape[0]
    squares = stay[row_count : row_count + 1, :] + whole(came[row_count:, :])
    inverse = lax.rsqrt(squares / D + epsilon) / math.sqrt(D)
    shape = (row_count, row_count)
    same = lax.broadcasted_iota(jnp.int32, shape, 0) == lax.broadcasted_iota(jnp.int32, shape, 1)
    inverse = jnp.sum(jnp.where(same, inverse, 0.0), axis=1, keepdims=True)
    scores[...] = ((stay[0:row_count, :] + came[0:row_count, :].astype(jnp.float32)) * inverse).astype(jnp.bfloat16)


def line_of_four(shape, gallery, neighbour, weights, send_rows, queries):
    groups, shards, blocks = shape
    row_count, col_count = gallery.shape
    query_count = queries.shape[0]
    half = query_count // 2
    cap = send_rows.shape[1] // shards
    low, high = jnp.bfloat16, jnp.float32

    def place(device):
        return (device[0] * shards + device[1]) * blocks + device[2]

    def send(value, to):
        pairs = []
        for g in range(groups):
            for z in range(shards):
                for q in range(blocks):
                    pairs.append((place((g, z, q)), place(to(g, z, q))))
        return lax.ppermute(value, AXES, pairs)

    to_third, to_first, to_second = call(
        functools.partial(pack_kernel, cap),
        [array((half + cap, col_count), low), array((half + cap, col_count), low), array((cap, col_count), low)],
        *(pltpu.with_memory_space_constraint(item, pltpu.HBM) for item in (queries, gallery, send_rows)),
        specs=[pl.BlockSpec(memory_space=pltpu.HBM)] * 3,
        scratch=[
            pltpu.VMEM(gallery.shape, low),
            pltpu.VMEM(send_rows.shape, jnp.int32),
            pltpu.VMEM((shards * cap, col_count), low),
            pltpu.SemaphoreType.DMA((4,)),
        ],
    )
    third = send(to_third, lambda g, z, q: (g, z ^ 3, q))
    first = send(to_first, lambda g, z, q: (g, z ^ 1, q))
    second_rows = send(to_second, lambda g, z, q: (g, z ^ 2, q))

    passed, second_rows = lax.optimization_barrier((third[0:half], second_rows))
    third_other = send(passed, lambda g, z, q: (1 - g, z, q))
    second = send(passed, lambda g, z, q: (g, z ^ 1, q))
    second_other = send(passed, lambda g, z, q: (1 - g, z ^ 1, q))
    first_other = send(first[0:half], lambda g, z, q: (1 - g, z, q))

    refined, squares = call(
        functools.partial(refine_kernel, cap),
        [array((row_count, col_count), low), array((SPARE, row_count), high)],
        gallery,
        neighbour.T,
        weights.T,
        first,
        second_rows,
        third,
    )
    early, early_give = call(
        early_kernel,
        [array((row_count, query_count), high), array((row_count + SPARE, query_count), low)],
        refined,
        squares,
        queries,
        first,
        first_other,
    )
    early_came = send(early_give, lambda g, z, q: (g, z, q ^ 1))
    late, late_give = call(
        late_kernel,
        [array((row_count, query_count), high), array((row_count, query_count), low)],
        refined,
        third,
        second_other,
        third_other,
        second,
    )
    late_came = send(late_give, lambda g, z, q: (g, z, q ^ 1))
    stay, leave = call(
        leave_kernel,
        [array((row_count + SPARE, query_count), high), array((row_count + SPARE, query_count), low)],
        early,
        early_came,
        squares,
        late,
        late_came,
    )
    came = send(leave, lambda g, z, q: (g, z, q ^ 2))
    (scores,) = call(score_kernel, [jax.ShapeDtypeStruct((row_count, query_count), low)], stay, came)
    return (refined, scores)


def solution(mesh):
    shape = tuple(mesh.shape[name] for name in AXES)

    def per_device(*arrays):
        if shape == (2, 4, 4):
            return line_of_four(shape, *arrays)
        return generic(*arrays)

    return jax.shard_map(
        per_device,
        mesh=mesh,
        in_specs=(
            P(("groups", "gallery"), "query"),
            P(("groups", "gallery"), None),
            P(("groups", "gallery"), None),
            P(("groups", "gallery"), None),
            P("gallery", "query"),
        ),
        out_specs=(P(("groups", "gallery"), "query"), P(("groups", "gallery"), "query")),
        check_vma=False,
    )
```

```python
import functools
import math

import jax
import jax.numpy as jnp
from jax import lax
from jax.experimental import pallas as pl
from jax.experimental.pallas import tpu as pltpu
from jax.sharding import PartitionSpec as P

D = 2048


self_weight = 4.0
epsilon = 1e-06

AXES = ("groups", "gallery", "query")


def weight_matrix(columns, neighbour, weights, width):
    row_count = neighbour.shape[0]
    places = lax.broadcasted_iota(jnp.int32, (row_count, width), 1)
    owners = lax.broadcasted_iota(jnp.int32, (row_count, width), 0)
    matrix = jnp.where(places == owners, jnp.int32(self_weight), 0)
    for which in range(neighbour.shape[1]):
        matrix = matrix + jnp.where(places == columns[:, which][:, None], weights[:, which][:, None], 0)
    return matrix.astype(jnp.bfloat16)


def dot_rows(left, right):
    return lax.dot_general(left, right, (((1,), (1,)), ((), ())), preferred_element_type=jnp.float32)


def generic(gallery, neighbour, weights, send_rows, queries):
    row_count = gallery.shape[0]
    arrived = lax.all_to_all(gallery[send_rows[0]], "gallery", split_axis=0, concat_axis=0, tiled=True)
    table = jnp.concatenate([gallery, arrived], axis=0)
    matrix = weight_matrix(neighbour, neighbour, weights, table.shape[0])
    summed = lax.dot_general(matrix, table, (((1,), (0,)), ((), ())), preferred_element_type=jnp.float32)
    denominator = self_weight + jnp.sum(weights.astype(jnp.float32), axis=1)
    refined = (summed / denominator[:, None]).astype(jnp.bfloat16)
    floats = refined.astype(jnp.float32)
    squares = lax.psum(jnp.sum(floats * floats, axis=1), "query")
    partial_value = dot_rows(refined, lax.all_gather(queries, "gallery", axis=0, tiled=True))
    raw = lax.psum_scatter(partial_value, "query", scatter_dimension=1, tiled=True)
    inverse = lax.rsqrt(squares / D + epsilon) / math.sqrt(D)
    return (refined, (raw * inverse[:, None]).astype(jnp.bfloat16))


VMEM = pl.BlockSpec(memory_space=pltpu.VMEM)
SPARE = 16


def call(kernel, outs, *operands, scratch=(), flops=0, specs=None):
    size = sum(math.prod(item.shape) * item.dtype.itemsize for item in (*outs, *operands))
    return pl.pallas_call(
        kernel,
        out_shape=list(outs),
        in_specs=specs or [VMEM] * len(operands),
        out_specs=[VMEM] * len(outs),
        scratch_shapes=list(scratch),
        compiler_params=pltpu.CompilerParams(vmem_limit_bytes=16 * 1024 * 1024),
        cost_estimate=pl.CostEstimate(flops=flops, bytes_accessed=size, transcendentals=0),
    )(*operands)


def array(shape, kind):
    return pltpu.VMEM(shape, kind)


def dot_columns(left, right):
    return lax.dot_general(left, right, (((0,), (0,)), ((), ())), preferred_element_type=jnp.float32)


def three_parts(row):
    high = row.astype(jnp.bfloat16).astype(jnp.float32)
    middle = (row - high).astype(jnp.bfloat16).astype(jnp.float32)
    low = row - high - middle
    index = lax.broadcasted_iota(jnp.int32, row.shape, 0)
    parts = jnp.where(index == 0, high, jnp.where(index == 1, middle, jnp.where(index == 2, low, 0.0)))
    return parts.astype(jnp.bfloat16)


def pack_kernel(
    cap, queries, gallery, send_rows, to_third, to_first, to_second, rows_in, lists_in, picked, arrived
):
    g, z = lax.axis_index("groups"), lax.axis_index("gallery")
    half = to_third.shape[0] - cap
    mine = queries.at[pl.ds(pl.multiple_of(g * half, half), half), :]
    copies = [
        pltpu.make_async_copy(send_rows, lists_in, arrived.at[0]),
        pltpu.make_async_copy(gallery, rows_in, arrived.at[1]),
        pltpu.make_async_copy(mine, to_third.at[0:half, :], arrived.at[2]),
        pltpu.make_async_copy(mine, to_first.at[0:half, :], arrived.at[3]),
    ]
    for copy in copies:
        copy.start()
    copies[0].wait()
    shape = (rows_in.shape[0], lists_in.shape[1])
    hot = jnp.where(lax.broadcasted_iota(jnp.int32, shape, 0) == lists_in[0:1, :], 1.0, 0.0).astype(jnp.bfloat16)
    copies[1].wait()
    picked[...] = dot_columns(hot, rows_in[...]).astype(jnp.bfloat16)

    def rows(step):
        return picked[pl.ds(pl.multiple_of(jnp.bitwise_xor(z, step) * cap, cap), cap), :]

    to_third[half:, :] = rows(3)
    to_first[half:, :] = rows(1)
    to_second[...] = rows(2)
    copies[2].wait()
    copies[3].wait()


def refine_kernel(cap, gallery, neighbour, weights, first, second, third, refined, squares):
    z = lax.axis_index("gallery")
    row_count, col_count = gallery.shape
    index = neighbour[...]
    weight = weights[...].astype(jnp.float32)
    slot = jnp.maximum(index - row_count, 0)
    far = (jnp.bitwise_xor(lax.div(slot, cap), z) - 1) * cap + lax.rem(slot, cap)
    far = jnp.where(index >= row_count, far, -1)

    def matrix(places, height, base):
        places_of = lax.broadcasted_iota(jnp.int32, (height, row_count), 0)
        total = base(places_of)
        for which in range(index.shape[0]):
            total = total + jnp.where(places_of == places[which : which + 1, :], weight[which : which + 1, :], 0.0)
        return total.astype(jnp.bfloat16)

    def own(places_of):
        return jnp.where(places_of == lax.broadcasted_iota(jnp.int32, places_of.shape, 1), self_weight, 0.0)

    near_matrix = matrix(index, row_count, own)
    far_matrix = matrix(far, 3 * cap, lambda places_of: jnp.zeros(places_of.shape, jnp.float32))
    half = first.shape[0] - cap
    table = jnp.concatenate([first[half:, :], second[...], third[half:, :]], axis=0)
    summed = dot_columns(near_matrix, gallery[...]) + dot_columns(far_matrix, table)
    denominator = dot_columns(near_matrix, jnp.ones((row_count, 128), jnp.bfloat16)) + dot_columns(
        far_matrix, jnp.ones((3 * cap, 128), jnp.bfloat16)
    )
    for start in range(0, col_count, 128):
        refined[:, start : start + 128] = (summed[:, start : start + 128] / denominator).astype(jnp.bfloat16)
    floats = refined[...].astype(jnp.float32)
    floats = floats * floats
    high = floats.astype(jnp.bfloat16)
    low = (floats - high.astype(jnp.float32)).astype(jnp.bfloat16)
    ones = jnp.ones((SPARE, col_count), jnp.bfloat16)
    squares[...] = dot_rows(ones, high) + dot_rows(ones, low)


def early_kernel(refined, squares, queries, first, first_other, keep, give):
    g, z, q = (lax.axis_index(name) for name in AXES)
    half = first_other.shape[0]
    row_count = refined.shape[0]
    odd = lax.rem(q + z, 2) == 1
    rows = refined[...]
    for place, one in ((g, first), (1 - g, first_other)):
        columns = pl.ds(pl.multiple_of(place * half, half), half)
        mine = queries[columns, :]
        came = one[0:half, :]
        keep[:, columns] = dot_rows(rows, jnp.where(odd, came, mine))
        give[0:row_count, columns] = dot_rows(rows, jnp.where(odd, mine, came)).astype(jnp.bfloat16)
    give[row_count:, :] = three_parts(squares[...])


def late_kernel(refined, third, second_other, third_other, second, keep, give):
    g, z, q = (lax.axis_index(name) for name in AXES)
    half = third_other.shape[0]
    odd = lax.rem(q + z, 2) == 1
    one = jnp.concatenate([third[0:half, :], third_other[...]], axis=0)
    two = jnp.concatenate([second[...], second_other[...]], axis=0)
    kept = dot_rows(refined[...], jnp.where(odd, one, two))
    given = dot_rows(refined[...], jnp.where(odd, two, one)).astype(jnp.bfloat16)
    for place, part in ((g, slice(0, half)), (1 - g, slice(half, 2 * half))):
        columns = pl.ds(pl.multiple_of(place * half, half), half)
        keep[:, columns] = kept[:, part]
        give[:, columns] = given[:, part]


def whole(parts):
    return jnp.sum(parts.astype(jnp.float32), axis=0, keepdims=True)


def leave_kernel(early, early_came, squares, late, late_came, stay, leave):
    z, q = lax.axis_index("gallery"), lax.axis_index("query")
    row_count = late.shape[0]
    near = lax.div(q, 2) == lax.div(z, 2)
    early_sum = early[...] + early_came[0:row_count, :].astype(jnp.float32)
    late_sum = late[...] + late_came[...].astype(jnp.float32)
    row = squares[...] + whole(early_came[row_count:, :])
    stay[0:row_count, :] = jnp.where(near, early_sum, late_sum)
    stay[row_count:, :] = row
    leave[0:row_count, :] = jnp.where(near, late_sum, early_sum).astype(jnp.bfloat16)
    leave[row_count:, :] = three_parts(row)


def score_kernel(stay, came, scores):
    row_count = scores.shape[0]
    squares = stay[row_count : row_count + 1, :] + whole(came[row_count:, :])
    inverse = lax.rsqrt(squares / D + epsilon) / math.sqrt(D)
    shape = (row_count, row_count)
    same = lax.broadcasted_iota(jnp.int32, shape, 0) == lax.broadcasted_iota(jnp.int32, shape, 1)
    inverse = jnp.sum(jnp.where(same, inverse, 0.0), axis=1, keepdims=True)
    scores[...] = ((stay[0:row_count, :] + came[0:row_count, :].astype(jnp.float32)) * inverse).astype(jnp.bfloat16)


def line_of_four(shape, gallery, neighbour, weights, send_rows, queries):
    groups, shards, blocks = shape
    row_count, col_count = gallery.shape
    query_count = queries.shape[0]
    half = query_count // 2
    cap = send_rows.shape[1] // shards
    low, high = jnp.bfloat16, jnp.float32

    def place(device):
        return (device[0] * shards + device[1]) * blocks + device[2]

    def send(value, to):
        pairs = []
        for g in range(groups):
            for z in range(shards):
                for q in range(blocks):
                    pairs.append((place((g, z, q)), place(to(g, z, q))))
        return lax.ppermute(value, AXES, pairs)

    to_third, to_first, to_second = call(
        functools.partial(pack_kernel, cap),
        [array((half + cap, col_count), low), array((half + cap, col_count), low), array((cap, col_count), low)],
        *(pltpu.with_memory_space_constraint(item, pltpu.HBM) for item in (queries, gallery, send_rows)),
        specs=[pl.BlockSpec(memory_space=pltpu.HBM)] * 3,
        scratch=[
            pltpu.VMEM(gallery.shape, low),
            pltpu.VMEM(send_rows.shape, jnp.int32),
            pltpu.VMEM((shards * cap, col_count), low),
            pltpu.SemaphoreType.DMA((4,)),
        ],
    )
    third = send(to_third, lambda g, z, q: (g, z ^ 3, q))
    first = send(to_first, lambda g, z, q: (g, z ^ 1, q))
    second_rows = send(to_second, lambda g, z, q: (g, z ^ 2, q))

    passed, second_rows = lax.optimization_barrier((third[0:half], second_rows))
    third_other = send(passed, lambda g, z, q: (1 - g, z, q))
    second = send(passed, lambda g, z, q: (g, z ^ 1, q))
    second_other = send(passed, lambda g, z, q: (1 - g, z ^ 1, q))
    first_other = send(first[0:half], lambda g, z, q: (1 - g, z, q))

    refined, squares = call(
        functools.partial(refine_kernel, cap),
        [array((row_count, col_count), low), array((SPARE, row_count), high)],
        gallery,
        neighbour.T,
        weights.T,
        first,
        second_rows,
        third,
    )
    early, early_give = call(
        early_kernel,
        [array((row_count, query_count), high), array((row_count + SPARE, query_count), low)],
        refined,
        squares,
        queries,
        first,
        first_other,
    )
    early_came = send(early_give, lambda g, z, q: (g, z, q ^ 1))
    late, late_give = call(
        late_kernel,
        [array((row_count, query_count), high), array((row_count, query_count), low)],
        refined,
        third,
        second_other,
        third_other,
        second,
    )
    late_came = send(late_give, lambda g, z, q: (g, z, q ^ 1))
    stay, leave = call(
        leave_kernel,
        [array((row_count + SPARE, query_count), high), array((row_count + SPARE, query_count), low)],
        early,
        early_came,
        squares,
        late,
        late_came,
    )
    came = send(leave, lambda g, z, q: (g, z, q ^ 2))
    (scores,) = call(score_kernel, [jax.ShapeDtypeStruct((row_count, query_count), low)], stay, came)
    return (refined, scores)


def solution(mesh):
    shape = tuple(mesh.shape[name] for name in AXES)

    def per_device(*arrays):
        if shape == (2, 4, 4):
            return line_of_four(shape, *arrays)
        return generic(*arrays)

    return jax.shard_map(
        per_device,
        mesh=mesh,
        in_specs=(
            P(("groups", "gallery"), "query"),
            P(("groups", "gallery"), None),
            P(("groups", "gallery"), None),
            P(("groups", "gallery"), None),
            P("gallery", "query"),
        ),
        out_specs=(P(("groups", "gallery"), "query"), P(("groups", "gallery"), "query")),
        check_vma=False,
    )
```

```python
import functools
import math

import jax
import jax.numpy as jnp
from jax import lax
from jax.experimental import pallas as pl
from jax.experimental.pallas import tpu as pltpu
from jax.sharding import PartitionSpec as P

D = 2048


self_weight = 4.0
epsilon = 1e-06

AXES = ("groups", "gallery", "query")


def weight_matrix(columns, neighbour, weights, width):
    row_count = neighbour.shape[0]
    places = lax.broadcasted_iota(jnp.int32, (row_count, width), 1)
    owners = lax.broadcasted_iota(jnp.int32, (row_count, width), 0)
    matrix = jnp.where(places == owners, jnp.int32(self_weight), 0)
    for which in range(neighbour.shape[1]):
        matrix = matrix + jnp.where(places == columns[:, which][:, None], weights[:, which][:, None], 0)
    return matrix.astype(jnp.bfloat16)


def dot_rows(left, right):
    return lax.dot_general(left, right, (((1,), (1,)), ((), ())), preferred_element_type=jnp.float32)


def generic(gallery, neighbour, weights, send_rows, queries):
    row_count = gallery.shape[0]
    arrived = lax.all_to_all(gallery[send_rows[0]], "gallery", split_axis=0, concat_axis=0, tiled=True)
    table = jnp.concatenate([gallery, arrived], axis=0)
    matrix = weight_matrix(neighbour, neighbour, weights, table.shape[0])
    summed = lax.dot_general(matrix, table, (((1,), (0,)), ((), ())), preferred_element_type=jnp.float32)
    denominator = self_weight + jnp.sum(weights.astype(jnp.float32), axis=1)
    refined = (summed / denominator[:, None]).astype(jnp.bfloat16)
    floats = refined.astype(jnp.float32)
    squares = lax.psum(jnp.sum(floats * floats, axis=1), "query")
    partial_value = dot_rows(refined, lax.all_gather(queries, "gallery", axis=0, tiled=True))
    raw = lax.psum_scatter(partial_value, "query", scatter_dimension=1, tiled=True)
    inverse = lax.rsqrt(squares / D + epsilon) / math.sqrt(D)
    return (refined, (raw * inverse[:, None]).astype(jnp.bfloat16))


VMEM = pl.BlockSpec(memory_space=pltpu.VMEM)
SPARE = 16


def call(kernel, outs, *operands, scratch=(), flops=0, specs=None, out_specs=None):
    size = sum(math.prod(item.shape) * item.dtype.itemsize for item in (*outs, *operands))
    return pl.pallas_call(
        kernel,
        out_shape=list(outs),
        in_specs=specs or [VMEM] * len(operands),
        out_specs=out_specs or [VMEM] * len(outs),
        scratch_shapes=list(scratch),
        compiler_params=pltpu.CompilerParams(vmem_limit_bytes=16 * 1024 * 1024),
        cost_estimate=pl.CostEstimate(flops=flops, bytes_accessed=size, transcendentals=0),
    )(*operands)


def array(shape, kind):
    return pltpu.VMEM(shape, kind)


def dot_columns(left, right):
    return lax.dot_general(left, right, (((0,), (0,)), ((), ())), preferred_element_type=jnp.float32)


def three_parts(row):
    high = row.astype(jnp.bfloat16).astype(jnp.float32)
    middle = (row - high).astype(jnp.bfloat16).astype(jnp.float32)
    low = row - high - middle
    index = lax.broadcasted_iota(jnp.int32, row.shape, 0)
    parts = jnp.where(index == 0, high, jnp.where(index == 1, middle, jnp.where(index == 2, low, 0.0)))
    return parts.astype(jnp.bfloat16)


def pack_kernel(
    cap, queries, gallery, send_rows, to_third, to_first, to_second, rows_in, lists_in, picked, arrived
):
    g, z = lax.axis_index("groups"), lax.axis_index("gallery")
    half = to_third.shape[0] - cap
    mine = queries.at[pl.ds(pl.multiple_of(g * half, half), half), :]
    copies = [
        pltpu.make_async_copy(send_rows, lists_in, arrived.at[0]),
        pltpu.make_async_copy(gallery, rows_in, arrived.at[1]),
        pltpu.make_async_copy(mine, to_third.at[0:half, :], arrived.at[2]),
        pltpu.make_async_copy(mine, to_first.at[0:half, :], arrived.at[3]),
    ]
    for index in (1, 0, 2, 3):
        copies[index].start()
    copies[0].wait()
    shape = (rows_in.shape[0], lists_in.shape[1])
    hot = jnp.where(lax.broadcasted_iota(jnp.int32, shape, 0) == lists_in[0:1, :], 1.0, 0.0).astype(jnp.bfloat16)
    copies[1].wait()
    picked[...] = dot_columns(hot, rows_in[...]).astype(jnp.bfloat16)

    def rows(step):
        return picked[pl.ds(pl.multiple_of(jnp.bitwise_xor(z, step) * cap, cap), cap), :]

    to_third[half:, :] = rows(3)
    to_first[half:, :] = rows(1)
    to_second[...] = rows(2)
    copies[2].wait()
    copies[3].wait()


def refine_kernel(cap, gallery, neighbour, weights, first, second, third, refined, squares):
    z = lax.axis_index("gallery")
    row_count, col_count = gallery.shape
    index = neighbour[...]
    weight = weights[...].astype(jnp.float32)
    slot = jnp.maximum(index - row_count, 0)
    far = (jnp.bitwise_xor(lax.div(slot, cap), z) - 1) * cap + lax.rem(slot, cap)
    far = jnp.where(index >= row_count, far, -1)

    def matrix(places, height, base):
        places_of = lax.broadcasted_iota(jnp.int32, (height, row_count), 0)
        total = base(places_of)
        for which in range(index.shape[0]):
            total = total + jnp.where(places_of == places[which : which + 1, :], weight[which : which + 1, :], 0.0)
        return total.astype(jnp.bfloat16)

    def own(places_of):
        return jnp.where(places_of == lax.broadcasted_iota(jnp.int32, places_of.shape, 1), self_weight, 0.0)

    near_matrix = matrix(index, row_count, own)
    far_matrix = matrix(far, 3 * cap, lambda places_of: jnp.zeros(places_of.shape, jnp.float32))
    half = first.shape[0] - cap
    table = jnp.concatenate([first[half:, :], second[...], third[half:, :]], axis=0)
    summed = dot_columns(near_matrix, gallery[...]) + dot_columns(far_matrix, table)
    denominator = dot_columns(near_matrix, jnp.ones((row_count, 128), jnp.bfloat16)) + dot_columns(
        far_matrix, jnp.ones((3 * cap, 128), jnp.bfloat16)
    )
    for start in range(0, col_count, 128):
        refined[:, start : start + 128] = (summed[:, start : start + 128] / denominator).astype(jnp.bfloat16)
    floats = refined[...].astype(jnp.float32)
    floats = floats * floats
    high = floats.astype(jnp.bfloat16)
    low = (floats - high.astype(jnp.float32)).astype(jnp.bfloat16)
    ones = jnp.ones((SPARE, col_count), jnp.bfloat16)
    squares[...] = dot_rows(ones, high) + dot_rows(ones, low)


def early_kernel(refined, squares, queries, first, first_other, keep, give):
    g, z, q = (lax.axis_index(name) for name in AXES)
    half = first_other.shape[0]
    row_count = refined.shape[0]
    odd = lax.rem(q + z, 2) == 1
    low = g == 0
    mine, other = first[0:half, :], first_other[...]
    came = jnp.concatenate([jnp.where(low, mine, other), jnp.where(low, other, mine)], axis=0)
    keep[...] = dot_rows(refined[...], jnp.where(odd, came, queries[...]))
    give[0:row_count, :] = dot_rows(refined[...], jnp.where(odd, queries[...], came)).astype(jnp.bfloat16)
    give[row_count:, :] = three_parts(squares[...])


def late_kernel(refined, third, second_other, third_other, second, keep, give):
    g, z, q = (lax.axis_index(name) for name in AXES)
    half = third_other.shape[0]
    odd = lax.rem(q + z, 2) == 1
    one = jnp.concatenate([third[0:half, :], third_other[...]], axis=0)
    two = jnp.concatenate([second[...], second_other[...]], axis=0)
    kept = dot_rows(refined[...], jnp.where(odd, one, two))
    given = dot_rows(refined[...], jnp.where(odd, two, one)).astype(jnp.bfloat16)
    for place, part in ((g, slice(0, half)), (1 - g, slice(half, 2 * half))):
        columns = pl.ds(pl.multiple_of(place * half, half), half)
        keep[:, columns] = kept[:, part]
        give[:, columns] = given[:, part]


def whole(parts):
    return jnp.sum(parts.astype(jnp.float32), axis=0, keepdims=True)


def leave_kernel(early, early_came, squares, late, late_came, stay, leave):
    z, q = lax.axis_index("gallery"), lax.axis_index("query")
    row_count = late.shape[0]
    near = lax.div(q, 2) == lax.div(z, 2)
    early_sum = early[...] + early_came[0:row_count, :].astype(jnp.float32)
    late_sum = late[...] + late_came[...].astype(jnp.float32)
    row = squares[...] + whole(early_came[row_count:, :])
    stay[0:row_count, :] = jnp.where(near, early_sum, late_sum)
    stay[row_count:, :] = row
    leave[0:row_count, :] = jnp.where(near, late_sum, early_sum).astype(jnp.bfloat16)
    leave[row_count:, :] = three_parts(row)


def score_kernel(stay, came, scores, held, sent):
    row_count = held.shape[0]
    part = row_count // 2
    squares = stay[row_count : row_count + 1, :] + whole(came[row_count:, :])
    inverse = lax.rsqrt(squares / D + epsilon) / math.sqrt(D)
    copies = []
    for index in range(2):
        rows = slice(index * part, (index + 1) * part)
        shape = (part, row_count)
        places = lax.broadcasted_iota(jnp.int32, shape, 0) + index * part
        same = places == lax.broadcasted_iota(jnp.int32, shape, 1)
        scale = jnp.sum(jnp.where(same, inverse, 0.0), axis=1, keepdims=True)
        held[rows, :] = ((stay[rows, :] + came[rows, :].astype(jnp.float32)) * scale).astype(jnp.bfloat16)
        copies.append(pltpu.make_async_copy(held.at[rows, :], scores.at[rows, :], sent.at[index]))
        copies[index].start()
    for copy in copies:
        copy.wait()


def line_of_four(shape, gallery, neighbour, weights, send_rows, queries):
    groups, shards, blocks = shape
    row_count, col_count = gallery.shape
    query_count = queries.shape[0]
    half = query_count // 2
    cap = send_rows.shape[1] // shards
    low, high = jnp.bfloat16, jnp.float32

    def place(device):
        return (device[0] * shards + device[1]) * blocks + device[2]

    def send(value, to):
        pairs = []
        for g in range(groups):
            for z in range(shards):
                for q in range(blocks):
                    pairs.append((place((g, z, q)), place(to(g, z, q))))
        return lax.ppermute(value, AXES, pairs)

    to_third, to_first, to_second = call(
        functools.partial(pack_kernel, cap),
        [array((half + cap, col_count), low), array((half + cap, col_count), low), array((cap, col_count), low)],
        *(pltpu.with_memory_space_constraint(item, pltpu.HBM) for item in (queries, gallery, send_rows)),
        specs=[pl.BlockSpec(memory_space=pltpu.HBM)] * 3,
        scratch=[
            pltpu.VMEM(gallery.shape, low),
            pltpu.VMEM(send_rows.shape, jnp.int32),
            pltpu.VMEM((shards * cap, col_count), low),
            pltpu.SemaphoreType.DMA((4,)),
        ],
    )
    third = send(to_third, lambda g, z, q: (g, z ^ 3, q))
    first = send(to_first, lambda g, z, q: (g, z ^ 1, q))
    second_rows = send(to_second, lambda g, z, q: (g, z ^ 2, q))

    passed, second_rows = lax.optimization_barrier((third[0:half], second_rows))
    third_other = send(passed, lambda g, z, q: (1 - g, z, q))
    second = send(passed, lambda g, z, q: (g, z ^ 1, q))
    second_other = send(passed, lambda g, z, q: (1 - g, z ^ 1, q))
    first_other = send(first[0:half], lambda g, z, q: (1 - g, z, q))

    refined, squares = call(
        functools.partial(refine_kernel, cap),
        [array((row_count, col_count), low), array((SPARE, row_count), high)],
        gallery,
        neighbour.T,
        weights.T,
        first,
        second_rows,
        third,
    )
    early, early_give = call(
        early_kernel,
        [array((row_count, query_count), high), array((row_count + SPARE, query_count), low)],
        refined,
        squares,
        queries,
        first,
        first_other,
    )
    early_came = send(early_give, lambda g, z, q: (g, z, q ^ 1))
    late, late_give = call(
        late_kernel,
        [array((row_count, query_count), high), array((row_count, query_count), low)],
        refined,
        third,
        second_other,
        third_other,
        second,
    )
    late_came = send(late_give, lambda g, z, q: (g, z, q ^ 1))
    stay, leave = call(
        leave_kernel,
        [array((row_count + SPARE, query_count), high), array((row_count + SPARE, query_count), low)],
        early,
        early_came,
        squares,
        late,
        late_came,
    )
    came = send(leave, lambda g, z, q: (g, z, q ^ 2))
    (scores,) = call(
        score_kernel,
        [jax.ShapeDtypeStruct((row_count, query_count), low)],
        stay,
        came,
        out_specs=[pl.BlockSpec(memory_space=pltpu.HBM)],
        scratch=[pltpu.VMEM((row_count, query_count), low), pltpu.SemaphoreType.DMA((2,))],
    )
    return (refined, scores)


def solution(mesh):
    shape = tuple(mesh.shape[name] for name in AXES)

    def per_device(*arrays):
        if shape == (2, 4, 4):
            return line_of_four(shape, *arrays)
        return generic(*arrays)

    return jax.shard_map(
        per_device,
        mesh=mesh,
        in_specs=(
            P(("groups", "gallery"), "query"),
            P(("groups", "gallery"), None),
            P(("groups", "gallery"), None),
            P(("groups", "gallery"), None),
            P("gallery", "query"),
        ),
        out_specs=(P(("groups", "gallery"), "query"), P(("groups", "gallery"), "query")),
        check_vma=False,
    )
```

```python
import functools
import math

import jax
import jax.numpy as jnp
from jax import lax
from jax.experimental import pallas as pl
from jax.experimental.pallas import tpu as pltpu
from jax.sharding import PartitionSpec as P

D = 2048


self_weight = 4.0
epsilon = 1e-06

AXES = ("groups", "gallery", "query")


def weight_matrix(columns, neighbour, weights, width):
    row_count = neighbour.shape[0]
    places = lax.broadcasted_iota(jnp.int32, (row_count, width), 1)
    owners = lax.broadcasted_iota(jnp.int32, (row_count, width), 0)
    matrix = jnp.where(places == owners, jnp.int32(self_weight), 0)
    for which in range(neighbour.shape[1]):
        matrix = matrix + jnp.where(places == columns[:, which][:, None], weights[:, which][:, None], 0)
    return matrix.astype(jnp.bfloat16)


def dot_rows(left, right):
    return lax.dot_general(left, right, (((1,), (1,)), ((), ())), preferred_element_type=jnp.float32)


def generic(gallery, neighbour, weights, send_rows, queries):
    row_count = gallery.shape[0]
    arrived = lax.all_to_all(gallery[send_rows[0]], "gallery", split_axis=0, concat_axis=0, tiled=True)
    table = jnp.concatenate([gallery, arrived], axis=0)
    matrix = weight_matrix(neighbour, neighbour, weights, table.shape[0])
    summed = lax.dot_general(matrix, table, (((1,), (0,)), ((), ())), preferred_element_type=jnp.float32)
    denominator = self_weight + jnp.sum(weights.astype(jnp.float32), axis=1)
    refined = (summed / denominator[:, None]).astype(jnp.bfloat16)
    floats = refined.astype(jnp.float32)
    squares = lax.psum(jnp.sum(floats * floats, axis=1), "query")
    partial_value = dot_rows(refined, lax.all_gather(queries, "gallery", axis=0, tiled=True))
    raw = lax.psum_scatter(partial_value, "query", scatter_dimension=1, tiled=True)
    inverse = lax.rsqrt(squares / D + epsilon) / math.sqrt(D)
    return (refined, (raw * inverse[:, None]).astype(jnp.bfloat16))


VMEM = pl.BlockSpec(memory_space=pltpu.VMEM)
SPARE = 16


def call(kernel, outs, *operands, scratch=(), flops=0, specs=None):
    size = sum(math.prod(item.shape) * item.dtype.itemsize for item in (*outs, *operands))
    return pl.pallas_call(
        kernel,
        out_shape=list(outs),
        in_specs=specs or [VMEM] * len(operands),
        out_specs=[VMEM] * len(outs),
        scratch_shapes=list(scratch),
        compiler_params=pltpu.CompilerParams(vmem_limit_bytes=16 * 1024 * 1024),
        cost_estimate=pl.CostEstimate(flops=flops, bytes_accessed=size, transcendentals=0),
    )(*operands)


def array(shape, kind):
    return pltpu.VMEM(shape, kind)


def dot_columns(left, right):
    return lax.dot_general(left, right, (((0,), (0,)), ((), ())), preferred_element_type=jnp.float32)


def three_parts(row):
    high = row.astype(jnp.bfloat16).astype(jnp.float32)
    middle = (row - high).astype(jnp.bfloat16).astype(jnp.float32)
    low = row - high - middle
    index = lax.broadcasted_iota(jnp.int32, row.shape, 0)
    parts = jnp.where(index == 0, high, jnp.where(index == 1, middle, jnp.where(index == 2, low, 0.0)))
    return parts.astype(jnp.bfloat16)


def pack_kernel(
    cap, queries, gallery, send_rows, to_third, to_first, to_second, rows_in, lists_in, picked, arrived
):
    g, z = lax.axis_index("groups"), lax.axis_index("gallery")
    half = to_third.shape[0] - cap
    mine = queries.at[pl.ds(pl.multiple_of(g * half, half), half), :]
    copies = [
        pltpu.make_async_copy(send_rows, lists_in, arrived.at[0]),
        pltpu.make_async_copy(gallery, rows_in, arrived.at[1]),
        pltpu.make_async_copy(mine, to_third.at[0:half, :], arrived.at[2]),
        pltpu.make_async_copy(mine, to_first.at[0:half, :], arrived.at[3]),
    ]
    for copy in copies:
        copy.start()
    copies[0].wait()
    shape = (rows_in.shape[0], lists_in.shape[1])
    hot = jnp.where(lax.broadcasted_iota(jnp.int32, shape, 0) == lists_in[0:1, :], 1.0, 0.0).astype(jnp.bfloat16)
    copies[1].wait()
    picked[...] = dot_columns(hot, rows_in[...]).astype(jnp.bfloat16)

    def rows(step):
        return picked[pl.ds(pl.multiple_of(jnp.bitwise_xor(z, step) * cap, cap), cap), :]

    to_third[half:, :] = rows(3)
    to_first[half:, :] = rows(1)
    to_second[...] = rows(2)
    copies[2].wait()
    copies[3].wait()


def refine_kernel(cap, gallery, neighbour, weights, first, second, third, refined, squares):
    z = lax.axis_index("gallery")
    row_count, col_count = gallery.shape
    index = neighbour[...]
    weight = weights[...].astype(jnp.float32)
    slot = jnp.maximum(index - row_count, 0)
    far = (jnp.bitwise_xor(lax.div(slot, cap), z) - 1) * cap + lax.rem(slot, cap)
    far = jnp.where(index >= row_count, far, -1)

    def matrix(places, height, base):
        places_of = lax.broadcasted_iota(jnp.int32, (height, row_count), 0)
        total = base(places_of)
        for which in range(index.shape[0]):
            total = total + jnp.where(places_of == places[which : which + 1, :], weight[which : which + 1, :], 0.0)
        return total.astype(jnp.bfloat16)

    def own(places_of):
        return jnp.where(places_of == lax.broadcasted_iota(jnp.int32, places_of.shape, 1), self_weight, 0.0)

    near_matrix = matrix(index, row_count, own)
    far_matrix = matrix(far, 3 * cap, lambda places_of: jnp.zeros(places_of.shape, jnp.float32))
    half = first.shape[0] - cap
    table = jnp.concatenate([first[half:, :], second[...], third[half:, :]], axis=0)
    summed = dot_columns(near_matrix, gallery[...]) + dot_columns(far_matrix, table)
    denominator = dot_columns(near_matrix, jnp.ones((row_count, 128), jnp.bfloat16)) + dot_columns(
        far_matrix, jnp.ones((3 * cap, 128), jnp.bfloat16)
    )
    for start in range(0, col_count, 128):
        refined[:, start : start + 128] = (summed[:, start : start + 128] / denominator).astype(jnp.bfloat16)
    floats = refined[...].astype(jnp.float32)
    floats = floats * floats
    high = floats.astype(jnp.bfloat16)
    low = (floats - high.astype(jnp.float32)).astype(jnp.bfloat16)
    ones = jnp.ones((SPARE, col_count), jnp.bfloat16)
    squares[...] = dot_rows(ones, high) + dot_rows(ones, low)


def early_kernel(refined, squares, queries, first, first_other, keep, give):
    g, z, q = (lax.axis_index(name) for name in AXES)
    half = first_other.shape[0]
    row_count = refined.shape[0]
    odd = lax.rem(q + z, 2) == 1
    low = g == 0
    mine, other = first[0:half, :], first_other[...]
    came = jnp.concatenate([jnp.where(low, mine, other), jnp.where(low, other, mine)], axis=0)
    keep[...] = dot_rows(refined[...], jnp.where(odd, came, queries[...]))
    give[0:row_count, :] = dot_rows(refined[...], jnp.where(odd, queries[...], came)).astype(jnp.bfloat16)
    give[row_count:, :] = three_parts(squares[...])


def late_kernel(refined, third, second_other, third_other, second, keep, give):
    g, z, q = (lax.axis_index(name) for name in AXES)
    half = third_other.shape[0]
    odd = lax.rem(q + z, 2) == 1
    one = jnp.concatenate([third[0:half, :], third_other[...]], axis=0)
    two = jnp.concatenate([second[...], second_other[...]], axis=0)
    kept = dot_rows(refined[...], jnp.where(odd, one, two))
    given = dot_rows(refined[...], jnp.where(odd, two, one)).astype(jnp.bfloat16)
    for place, part in ((g, slice(0, half)), (1 - g, slice(half, 2 * half))):
        columns = pl.ds(pl.multiple_of(place * half, half), half)
        keep[:, columns] = kept[:, part]
        give[:, columns] = given[:, part]


def whole(parts):
    return jnp.sum(parts.astype(jnp.float32), axis=0, keepdims=True)


def leave_kernel(late, late_came, early, early_came, squares, stay, leave):
    z, q = lax.axis_index("gallery"), lax.axis_index("query")
    row_count = late.shape[0]
    near = lax.div(q, 2) == lax.div(z, 2)
    early_sum = early[...] + early_came[0:row_count, :].astype(jnp.float32)
    late_sum = late[...] + late_came[...].astype(jnp.float32)
    row = squares[...] + whole(early_came[row_count:, :])
    stay[0:row_count, :] = jnp.where(near, early_sum, late_sum)
    stay[row_count:, :] = row
    leave[0:row_count, :] = jnp.where(near, late_sum, early_sum).astype(jnp.bfloat16)
    leave[row_count:, :] = three_parts(row)


def score_kernel(stay, came, scores):
    row_count = scores.shape[0]
    squares = stay[row_count : row_count + 1, :] + whole(came[row_count:, :])
    inverse = lax.rsqrt(squares / D + epsilon) / math.sqrt(D)
    shape = (row_count, row_count)
    same = lax.broadcasted_iota(jnp.int32, shape, 0) == lax.broadcasted_iota(jnp.int32, shape, 1)
    inverse = jnp.sum(jnp.where(same, inverse, 0.0), axis=1, keepdims=True)
    scores[...] = ((stay[0:row_count, :] + came[0:row_count, :].astype(jnp.float32)) * inverse).astype(jnp.bfloat16)


def line_of_four(shape, gallery, neighbour, weights, send_rows, queries):
    groups, shards, blocks = shape
    row_count, col_count = gallery.shape
    query_count = queries.shape[0]
    half = query_count // 2
    cap = send_rows.shape[1] // shards
    low, high = jnp.bfloat16, jnp.float32

    def place(device):
        return (device[0] * shards + device[1]) * blocks + device[2]

    def send(value, to):
        pairs = []
        for g in range(groups):
            for z in range(shards):
                for q in range(blocks):
                    pairs.append((place((g, z, q)), place(to(g, z, q))))
        return lax.ppermute(value, AXES, pairs)

    to_third, to_first, to_second = call(
        functools.partial(pack_kernel, cap),
        [array((half + cap, col_count), low), array((half + cap, col_count), low), array((cap, col_count), low)],
        *(pltpu.with_memory_space_constraint(item, pltpu.HBM) for item in (queries, gallery, send_rows)),
        specs=[pl.BlockSpec(memory_space=pltpu.HBM)] * 3,
        scratch=[
            pltpu.VMEM(gallery.shape, low),
            pltpu.VMEM(send_rows.shape, jnp.int32),
            pltpu.VMEM((shards * cap, col_count), low),
            pltpu.SemaphoreType.DMA((4,)),
        ],
    )
    third = send(to_third, lambda g, z, q: (g, z ^ 3, q))
    first = send(to_first, lambda g, z, q: (g, z ^ 1, q))
    second_rows = send(to_second, lambda g, z, q: (g, z ^ 2, q))

    passed, second_rows = lax.optimization_barrier((third[0:half], second_rows))
    third_other = send(passed, lambda g, z, q: (1 - g, z, q))
    second = send(passed, lambda g, z, q: (g, z ^ 1, q))
    second_other = send(passed, lambda g, z, q: (1 - g, z ^ 1, q))
    first_other = send(first[0:half], lambda g, z, q: (1 - g, z, q))

    refined, squares = call(
        functools.partial(refine_kernel, cap),
        [array((row_count, col_count), low), array((SPARE, row_count), high)],
        gallery,
        neighbour.T,
        weights.T,
        first,
        second_rows,
        third,
    )
    early, early_give = call(
        early_kernel,
        [array((row_count, query_count), high), array((row_count + SPARE, query_count), low)],
        refined,
        squares,
        queries,
        first,
        first_other,
    )
    early_came = send(early_give, lambda g, z, q: (g, z, q ^ 1))
    late, late_give = call(
        late_kernel,
        [array((row_count, query_count), high), array((row_count, query_count), low)],
        refined,
        third,
        second_other,
        third_other,
        second,
    )
    late_came = send(late_give, lambda g, z, q: (g, z, q ^ 1))
    stay, leave = call(
        leave_kernel,
        [array((row_count + SPARE, query_count), high), array((row_count + SPARE, query_count), low)],
        late,
        late_came,
        early,
        early_came,
        squares,
    )
    came = send(leave, lambda g, z, q: (g, z, q ^ 2))
    (scores,) = call(score_kernel, [jax.ShapeDtypeStruct((row_count, query_count), low)], stay, came)
    return (refined, scores)


def solution(mesh):
    shape = tuple(mesh.shape[name] for name in AXES)

    def per_device(*arrays):
        if shape == (2, 4, 4):
            return line_of_four(shape, *arrays)
        return generic(*arrays)

    return jax.shard_map(
        per_device,
        mesh=mesh,
        in_specs=(
            P(("groups", "gallery"), "query"),
            P(("groups", "gallery"), None),
            P(("groups", "gallery"), None),
            P(("groups", "gallery"), None),
            P("gallery", "query"),
        ),
        out_specs=(P(("groups", "gallery"), "query"), P(("groups", "gallery"), "query")),
        check_vma=False,
    )
```
